256 devices in a mesh: seq: 64 (over z, y_lo, x), ch: 4 (over y_hi, core).
Axes of the slice: x: 4, y: 4 (y_hi: 2, y_lo: 2; y = y_hi * 2 + y_lo), z: 8, core: 2. Of those that a mesh axis runs over, the one named last changes fastest.
Arguments:
- query_gate: float32 [16384, 4096], P('seq', 'ch'), may hold values from -6 to 6
- key_gate: float32 [16384, 4096], P('seq', 'ch'), may hold values from -6 to 6
- value_in: float32 [16384, 4096], P('seq', 'ch'), may hold values from -6 to 6
- filters: float32 [2048, 4096], P('seq', 'ch'), may hold values from -2 to 2
- skip_gain: float32 [4096], P('ch'), may hold values from 0.1 to 1.9
Outputs:
- output: float32 [16384, 4096], P('seq', 'ch')
The draws below stay inside these ranges and needn't reach their ends.
All inputs are finite; a program needn't handle non-finite values.
Results may differ from the reference program's by a relative error of at most 0.0003.
Values sent between devices are 32-bit elements; how exact they have to be, the bound alone decides.
A program may use at most 128 MiB of HBM per device.

```python
import jax
import jax.numpy as jnp

D = 4096
TOKENS = 16384
FILT = 2048


def envelope(rates):
    lags = jnp.arange(FILT).astype(jnp.float32)
    ratio = jnp.exp(-rates)
    scale = jnp.sqrt((1.0 - ratio * ratio) / (1.0 - jnp.exp(-2.0 * rates * FILT)))
    return jnp.exp(-lags[:, None] * rates[None, :]) * scale[None, :]


def draw_filters(key, part):
    key = jax.random.fold_in(key, 7)
    rate_key, amp_key, slow_key, slow_amp_key = jax.random.split(key, 4)
    low = jnp.log(0.2 / FILT)
    high = jnp.log(1.0 / 30.0)
    rates = jnp.exp(jax.random.uniform(rate_key, (D,), jnp.float32, low, high))
    slow_rates = jnp.exp(jax.random.uniform(slow_key, (D,), jnp.float32, jnp.log(0.1 / FILT), jnp.log(1.0 / FILT)))
    amps = jnp.clip(jax.random.normal(amp_key, (FILT, D), jnp.float32), -6.0, 6.0)
    slow_amps = jnp.clip(jax.random.normal(slow_amp_key, (FILT, D), jnp.float32), -6.0, 6.0)
    return 0.95 * amps * envelope(rates) + 0.3 * slow_amps * envelope(slow_rates)


def shard_levels(own_key, extent, cuts, least, high):
    def one(axis_at, parts):
        heights = jax.random.uniform(jax.random.fold_in(jax.random.fold_in(own_key, 6), axis_at), (parts,), jnp.float32, least / len(cuts), high / len(cuts))
        return jnp.repeat(jnp.exp(heights), extent[axis_at] // parts).reshape((-1,) + (1,) * (len(extent) - axis_at - 1))

    loudness = one(*cuts[0])
    for cut in cuts[1:]:
        loudness = loudness * one(*cut)
    return loudness


def bell_draw(own_key, extent, width, reach, shards=(), held_as=jnp.bfloat16):
    values = jax.random.normal(own_key, extent, jnp.float32) * width
    if len(shards) > 0:
        values = shard_levels(own_key, extent, shards, -0.22, 0.18) * values
    return jnp.clip(values, min=-reach, max=reach).astype(held_as)


def setup_inputs(seed: int = 0) -> dict:
    seeds = jax.random.split(jax.random.key(seed), 6)
    query_gate = bell_draw(seeds[0], (TOKENS, D), 1.0, 6.0, ((0, 64), (1, 4)), jnp.float32)
    key_gate = bell_draw(seeds[1], (TOKENS, D), 1.0, 6.0, ((0, 64), (1, 4)), jnp.float32)
    value_in = bell_draw(seeds[2], (TOKENS, D), 1.0, 6.0, ((0, 64), (1, 4)), jnp.float32)
    filters = draw_filters(jax.random.fold_in(seeds[5], 71), 0)
    skip_gain = jnp.clip(1.0 + 0.18 * jax.random.normal(seeds[4], (D,), jnp.float32), 0.1, 1.9)
    return dict(query_gate=query_gate, key_gate=key_gate, value_in=value_in, filters=filters, skip_gain=skip_gain)


def reference(query_gate, key_gate, value_in, filters, skip_gain):
    mixed = key_gate * value_in
    length = TOKENS + FILT
    spec_in = jnp.fft.rfft(mixed, n=length, axis=0)
    spec_filt = jnp.fft.rfft(filters, n=length, axis=0)
    conv = jnp.fft.irfft(spec_in * spec_filt, n=length, axis=0)[:TOKENS]
    return query_gate * (conv + skip_gain[None, :] * mixed)
```

```python
import functools

import jax
import jax.numpy as jnp
import numpy as np
from jax import lax
from jax.experimental import pallas as pl
from jax.experimental.pallas import tpu as pltpu
from jax.sharding import PartitionSpec as P

MESH = pl.DeviceIdType.MESH
F32 = jnp.float32
BF16 = jnp.bfloat16
ROWS = 256
LANES = 128
NX, NY, NZ = 4, 2, 8
GROUP = NX * NY
LAGS = ROWS // GROUP
SPEC = 2 * ROWS
PIECES = 2
OFFSETS = [(0, 1), (0, 3), (1, 0), (1, 1), (1, 3), (0, 2), (1, 2)]


def tables():
    m = np.arange(ROWS)
    t = np.arange(ROWS)
    angle = np.pi * (((4 * m[:, None] + 1) * t[None, :]) % (4 * ROWS)) / (2 * ROWS)
    forward = np.concatenate([np.cos(angle), -np.sin(angle)], axis=0)
    back = np.concatenate([-np.sin(angle.T), -np.cos(angle.T)], axis=1) / ROWS
    split = []
    for table in (forward, back):
        high = table.astype(np.float32).astype(jnp.bfloat16)
        low = (table - high.astype(np.float64)).astype(np.float32).astype(jnp.bfloat16)
        split += [high, low]
    return split


def split(value):
    high = value.astype(BF16)
    low = (value - high.astype(F32)).astype(BF16)
    return high, low


def multiply(high_ref, low_ref, value):
    high, low = split(value)
    first = jnp.dot(high_ref[...], jnp.concatenate([high, low], axis=1), preferred_element_type=F32)
    second = jnp.dot(low_ref[...], high, preferred_element_type=F32)
    return first[:, :LANES] + first[:, LANES:] + second


def kernel(
    k_in, v_in, q_in, f_in, s_in, ch_in, cl_in, gh_in, gl_in, out_ref,
    k, v, q, f, s, ch, cl, gh, gl, mix, x, fb, y, fy, w, acc, send, got, out,
    load_sem, fs_sem, fr_sem, ms_sem, mr_sem, hs_sem, hr_sem, rs_sem, rr_sem, os_sem, or_sem, st_sem,
):
    seq = lax.axis_index("seq")
    z, d = seq // GROUP, seq % GROUP
    yy, xx = d // NX, d % NX
    above = ((z + 1) % NZ) * GROUP + d
    below = ((z + NZ - 1) % NZ) * GROUP + d

    def to(o):
        return ((yy + o[0]) % NY) * NX + (xx + o[1]) % NX

    def source(o):
        return ((yy + NY - o[0]) % NY) * NX + (xx + NX - o[1]) % NX

    def remote(src, dst, send_sem, recv_sem, dev):
        return pltpu.make_async_remote_copy(
            src_ref=src, dst_ref=dst, send_sem=send_sem, recv_sem=recv_sem,
            device_id={"seq": dev}, device_id_type=MESH,
        )

    def columns(p):
        return pl.ds(pl.multiple_of(p * LANES, LANES), LANES)

    loads = []
    for i, (a, b) in enumerate(
        [(f_in, f), (k_in, k), (v_in, v), (ch_in, ch), (cl_in, cl), (gh_in, gh), (gl_in, gl), (q_in, q), (s_in, s)]
    ):
        c = pltpu.make_async_copy(a, b, load_sem.at[i])
        c.start()
        loads.append(c)

    barrier = pltpu.get_barrier_semaphore()
    for o in OFFSETS:
        pl.semaphore_signal(barrier, inc=1, device_id={"seq": z * GROUP + to(o)}, device_id_type=MESH)
    for dev in (above, below):
        pl.semaphore_signal(barrier, inc=1, device_id={"seq": dev}, device_id_type=MESH)

    loads[0].wait()
    fb[z, pl.ds(pl.multiple_of(d * LAGS, LAGS), LAGS), :] = f[:, columns(d)]
    loads[1].wait()
    loads[2].wait()
    for p in range(GROUP):
        cols = slice(p * LANES, (p + 1) * LANES)
        mix[p] = k[:, cols] * v[:, cols]
    x[GROUP + d] = mix[d]
    pl.semaphore_wait(barrier, GROUP + 1)

    f_copies, m_copies = [], []
    for n, o in enumerate(OFFSETS):
        p = to(o)
        c = remote(
            f.at[:, columns(p)], fb.at[z, pl.ds(pl.multiple_of(d * LAGS, LAGS), LAGS)],
            fs_sem.at[n], fr_sem.at[n], z * GROUP + p,
        )
        c.start()
        f_copies.append(c)
    h_copies = []

    def halo(n, j):
        c = remote(x.at[GROUP + j], x.at[j], hs_sem.at[n], hr_sem.at[n], above)
        c.start()
        h_copies.append(c)

    halo(GROUP - 1, d)
    for n, o in enumerate(OFFSETS):
        p = to(o)
        c = remote(mix.at[p], x.at[GROUP + d], ms_sem.at[n], mr_sem.at[n], z * GROUP + p)
        c.start()
        m_copies.append(c)

    part = ROWS // PIECES
    r_copies = {}

    def hop(h, i):
        at = pl.ds(i * part, part)
        block = (z + h) % NZ
        c = remote(
            fb.at[block, at], fb.at[block, at], rs_sem.at[h * PIECES + i], rr_sem.at[h * PIECES + i], below
        )
        c.start()
        r_copies[h, i] = c

    def relay(h):
        for i in range(PIECES):
            r_copies[h, i].wait_recv()
            if h + 1 < NZ - 1:
                hop(h + 1, i)

    def arrive(n):
        m_copies[n].wait_recv()
        halo(n, source(OFFSETS[n]))

    def forward(src, block, dst, at):
        dst[at] = multiply(ch, cl, src[block])

    for c in f_copies:
        c.wait_recv()
    for i in range(PIECES):
        hop(0, i)
    for c in loads[3:]:
        c.wait()

    own = GROUP + d
    forward(x, own, y, own)
    forward(fb, z, fy, z)
    for h, group in enumerate([(0, 1), (2, 3), (4, 5), (6,)]):
        for n in group:
            arrive(n)
            j = GROUP + source(OFFSETS[n])
            forward(x, j, y, j)
        relay(h)
        block = (z + h + 1) % NZ
        forward(fb, block, fy, block)

    inside = (z > 0).astype(F32)

    def take(n, j):
        h_copies_by_slot[n].wait_recv()
        y[j] = multiply(ch, cl, x[j] * inside)

    h_copies_by_slot = {}
    for n, c in zip([GROUP - 1] + list(range(GROUP - 1)), h_copies):
        h_copies_by_slot[n] = c

    take(GROUP - 1, d)
    take(0, source(OFFSETS[0]))
    for h in range(4, NZ - 1):
        relay(h)
        block = (z + h + 1) % NZ
        forward(fb, block, fy, block)
        n = h - 3
        take(n, source(OFFSETS[n]))
    for n in range(4, GROUP - 1):
        take(n, source(OFFSETS[n]))

    def window(n, carry):
        def tile(r, carry):
            at = pl.ds(pl.multiple_of(r * 16, 16), 16)
            im = pl.ds(pl.multiple_of(r * 16 + ROWS, 16), 16)
            w[n, at] = y[n, at] + y[n + 1, im]
            w[n, im] = y[n, im] - y[n + 1, at]
            return carry

        return lax.fori_loop(0, ROWS // 16, tile, carry)

    lax.fori_loop(0, 2 * GROUP - 1, window, 0)

    def output(i):
        def tile(r, carry):
            at = pl.ds(pl.multiple_of(r * 8, 8), 8)
            im = pl.ds(pl.multiple_of(r * 8 + ROWS, 8), 8)
            real = jnp.zeros((8, LANES), F32)
            imag = jnp.zeros((8, LANES), F32)
            for j in range(GROUP):
                n = i + GROUP - 1 - j
                fr, fi = fy[j, at], fy[j, im]
                wr, wi = w[n, at], w[n, im]
                real += fr * wr - fi * wi
                imag += fr * wi + fi * wr
            acc[at] = real
            acc[im] = imag
            return carry

        lax.fori_loop(0, ROWS // 8, tile, 0, unroll=2)
        return multiply(gh, gl, acc[...])

    o_copies = []
    for n, o in enumerate(OFFSETS):
        p = to(o)
        send[n] = output(p)
        c = remote(send.at[n], got.at[d], os_sem.at[n], or_sem.at[n], z * GROUP + p)
        c.start()
        o_copies.append(c)
    got[d] = output(d)

    stores = []

    def finish(n, p):
        cols = columns(p)
        out[:, cols] = q[:, cols] * (got[p] + s[:, cols] * mix[p])
        c = pltpu.make_async_copy(out.at[:, cols], out_ref.at[:, cols], st_sem.at[n])
        c.start()
        stores.append(c)

    finish(GROUP - 1, d)
    for n, o in enumerate(OFFSETS):
        o_copies[n].wait_recv()
        finish(n, source(o))
    for c in f_copies + m_copies + h_copies + list(r_copies.values()) + o_copies:
        c.wait_send()
    for c in stores:
        c.wait()


def on_device(query_gate, key_gate, value_in, filters, skip_gain):
    width = GROUP * LANES
    hops = (NZ - 1) * PIECES
    arrays = [jnp.asarray(t) for t in tables()]
    vm = pltpu.VMEM
    dma = pltpu.SemaphoreType.DMA
    return pl.pallas_call(
        kernel,
        name="hyena",
        out_shape=jax.ShapeDtypeStruct((ROWS, width), F32),
        in_specs=[pl.BlockSpec(memory_space=pl.ANY)] * 9,
        out_specs=pl.BlockSpec(memory_space=pl.ANY),
        scratch_shapes=[
            vm((ROWS, width), F32),
            vm((ROWS, width), F32),
            vm((ROWS, width), F32),
            vm((LAGS, width), F32),
            vm((1, width), F32),
            vm((SPEC, ROWS), BF16),
            vm((SPEC, ROWS), BF16),
            vm((ROWS, SPEC), BF16),
            vm((ROWS, SPEC), BF16),
            vm((GROUP, ROWS, LANES), F32),
            vm((2 * GROUP, ROWS, LANES), F32),
            vm((NZ, ROWS, LANES), F32),
            vm((2 * GROUP, SPEC, LANES), F32),
            vm((NZ, SPEC, LANES), F32),
            vm((2 * GROUP - 1, SPEC, LANES), F32),
            vm((SPEC, LANES), F32),
            vm((GROUP - 1, ROWS, LANES), F32),
            vm((GROUP, ROWS, LANES), F32),
            vm((ROWS, width), F32),
            dma((9,)),
            dma((GROUP - 1,)), dma((GROUP - 1,)),
            dma((GROUP - 1,)), dma((GROUP - 1,)),
            dma((GROUP,)), dma((GROUP,)),
            dma((hops,)), dma((hops,)),
            dma((GROUP - 1,)), dma((GROUP - 1,)),
            dma((GROUP,)),
        ],
        compiler_params=pltpu.CompilerParams(
            collective_id=0, has_side_effects=True, vmem_limit_bytes=48 << 20
        ),
    )(key_gate, value_in, query_gate, filters, skip_gain.reshape(1, width), *arrays)


def solution(mesh):
    in_specs = (P("seq", "ch"), P("seq", "ch"), P("seq", "ch"), P("seq", "ch"), P("ch"))
    return jax.shard_map(
        on_device, mesh=mesh, in_specs=in_specs, out_specs=P("seq", "ch"), check_vma=False
    )
```

```python
import functools

import jax
import jax.numpy as jnp
import numpy as np
from jax import lax
from jax.experimental import pallas as pl
from jax.experimental.pallas import tpu as pltpu
from jax.sharding import PartitionSpec as P

MESH = pl.DeviceIdType.MESH
F32 = jnp.float32
BF16 = jnp.bfloat16
ROWS = 256
LANES = 128
NX, NY, NZ = 4, 2, 8
GROUP = NX * NY
LAGS = ROWS // GROUP
SPEC = 2 * ROWS
PIECES = 2
OFFSETS = [(0, 1), (0, 3), (1, 0), (1, 1), (1, 3), (0, 2), (1, 2)]


def tables():
    m = np.arange(ROWS)
    t = np.arange(ROWS)
    angle = np.pi * (((4 * m[:, None] + 1) * t[None, :]) % (4 * ROWS)) / (2 * ROWS)
    forward = np.concatenate([np.cos(angle), -np.sin(angle)], axis=0)
    back = np.concatenate([-np.sin(angle.T), -np.cos(angle.T)], axis=1) / ROWS
    split = []
    for table in (forward, back):
        high = table.astype(np.float32).astype(jnp.bfloat16)
        low = (table - high.astype(np.float64)).astype(np.float32).astype(jnp.bfloat16)
        split += [high, low]
    return split


def split(value):
    high = value.astype(BF16)
    low = (value - high.astype(F32)).astype(BF16)
    return high, low


def multiply(high_ref, low_ref, value):
    high, low = split(value)
    first = jnp.dot(high_ref[...], jnp.concatenate([high, low], axis=1), preferred_element_type=F32)
    second = jnp.dot(low_ref[...], high, preferred_element_type=F32)
    return first[:, :LANES] + first[:, LANES:] + second


def kernel(
    k_in, v_in, q_in, f_in, s_in, ch_in, cl_in, gh_in, gl_in, out_ref,
    k, v, q, f, s, ch, cl, gh, gl, mix, x, fb, y, fy, w, acc, send, got, out,
    load_sem, fs_sem, fr_sem, ms_sem, mr_sem, hs_sem, hr_sem, rs_sem, rr_sem, os_sem, or_sem, st_sem,
):
    seq = lax.axis_index("seq")
    z, d = seq // GROUP, seq % GROUP
    yy, xx = d // NX, d % NX
    above = ((z + 1) % NZ) * GROUP + d
    below = ((z + NZ - 1) % NZ) * GROUP + d

    def to(o):
        return ((yy + o[0]) % NY) * NX + (xx + o[1]) % NX

    def source(o):
        return ((yy + NY - o[0]) % NY) * NX + (xx + NX - o[1]) % NX

    def remote(src, dst, send_sem, recv_sem, dev):
        return pltpu.make_async_remote_copy(
            src_ref=src, dst_ref=dst, send_sem=send_sem, recv_sem=recv_sem,
            device_id={"seq": dev}, device_id_type=MESH,
        )

    def columns(p):
        return pl.ds(pl.multiple_of(p * LANES, LANES), LANES)

    loads = []
    for i, (a, b) in enumerate(
        [(f_in, f), (k_in, k), (v_in, v), (ch_in, ch), (cl_in, cl), (gh_in, gh), (gl_in, gl), (q_in, q), (s_in, s)]
    ):
        c = pltpu.make_async_copy(a, b, load_sem.at[i])
        c.start()
        loads.append(c)

    barrier = pltpu.get_barrier_semaphore()
    for o in OFFSETS:
        pl.semaphore_signal(barrier, inc=1, device_id={"seq": z * GROUP + to(o)}, device_id_type=MESH)
    for dev in (above, below):
        pl.semaphore_signal(barrier, inc=1, device_id={"seq": dev}, device_id_type=MESH)

    loads[0].wait()
    fb[z, pl.ds(pl.multiple_of(d * LAGS, LAGS), LAGS), :] = f[:, columns(d)]
    loads[1].wait()
    loads[2].wait()
    for p in range(GROUP):
        cols = slice(p * LANES, (p + 1) * LANES)
        mix[p] = k[:, cols] * v[:, cols]
    x[GROUP + d] = mix[d]
    pl.semaphore_wait(barrier, GROUP + 1)

    f_copies, m_copies = [], []
    for n, o in enumerate(OFFSETS):
        p = to(o)
        c = remote(
            f.at[:, columns(p)], fb.at[z, pl.ds(pl.multiple_of(d * LAGS, LAGS), LAGS)],
            fs_sem.at[n], fr_sem.at[n], z * GROUP + p,
        )
        c.start()
        f_copies.append(c)
    h_copies = []

    def halo(n, j):
        c = remote(x.at[GROUP + j], x.at[j], hs_sem.at[n], hr_sem.at[n], above)
        c.start()
        h_copies.append(c)

    halo(GROUP - 1, d)
    for n, o in enumerate(OFFSETS):
        p = to(o)
        c = remote(mix.at[p], x.at[GROUP + d], ms_sem.at[n], mr_sem.at[n], z * GROUP + p)
        c.start()
        m_copies.append(c)

    part = ROWS // PIECES
    r_copies = {}

    def hop(h, i):
        at = pl.ds(i * part, part)
        block = (z + h) % NZ
        c = remote(
            fb.at[block, at], fb.at[block, at], rs_sem.at[h * PIECES + i], rr_sem.at[h * PIECES + i], below
        )
        c.start()
        r_copies[h, i] = c

    def relay(h):
        for i in range(PIECES):
            r_copies[h, i].wait_recv()
            if h + 1 < NZ - 1:
                hop(h + 1, i)

    def arrive(n):
        m_copies[n].wait_recv()
        halo(n, source(OFFSETS[n]))

    def forward(src, block, dst, at):
        dst[at] = multiply(ch, cl, src[block])

    for c in f_copies:
        c.wait_recv()
    for i in range(PIECES):
        hop(0, i)
    for c in loads[3:]:
        c.wait()

    own = GROUP + d
    forward(x, own, y, own)
    forward(fb, z, fy, z)
    for h, group in enumerate([(0, 1), (2, 3), (4, 5), (6,)]):
        for n in group:
            arrive(n)
            j = GROUP + source(OFFSETS[n])
            forward(x, j, y, j)
        relay(h)
        block = (z + h + 1) % NZ
        forward(fb, block, fy, block)

    inside = (z > 0).astype(F32)

    def take(n, j):
        h_copies_by_slot[n].wait_recv()
        y[j] = multiply(ch, cl, x[j] * inside)

    h_copies_by_slot = {}
    for n, c in zip([GROUP - 1] + list(range(GROUP - 1)), h_copies):
        h_copies_by_slot[n] = c

    take(GROUP - 1, d)
    take(0, source(OFFSETS[0]))
    for h in range(4, NZ - 1):
        relay(h)
        block = (z + h + 1) % NZ
        forward(fb, block, fy, block)
        n = h - 3
        take(n, source(OFFSETS[n]))
    for n in range(4, GROUP - 1):
        take(n, source(OFFSETS[n]))

    def window(n, carry):
        def tile(r, carry):
            at = pl.ds(pl.multiple_of(r * 16, 16), 16)
            im = pl.ds(pl.multiple_of(r * 16 + ROWS, 16), 16)
            w[n, at] = y[n, at] + y[n + 1, im]
            w[n, im] = y[n, im] - y[n + 1, at]
            return carry

        return lax.fori_loop(0, ROWS // 16, tile, carry)

    lax.fori_loop(0, 2 * GROUP - 1, window, 0)

    def output(i):
        def tile(r, carry):
            at = pl.ds(pl.multiple_of(r * 8, 8), 8)
            im = pl.ds(pl.multiple_of(r * 8 + ROWS, 8), 8)
            real = jnp.zeros((8, LANES), F32)
            imag = jnp.zeros((8, LANES), F32)
            for j in range(GROUP):
                n = i + GROUP - 1 - j
                fr, fi = fy[j, at], fy[j, im]
                wr, wi = w[n, at], w[n, im]
                real += fr * wr - fi * wi
                imag += fr * wi + fi * wr
            acc[at] = real
            acc[im] = imag
            return carry

        lax.fori_loop(0, ROWS // 8, tile, 0, unroll=2)
        return multiply(gh, gl, acc[...])

    o_copies = []
    for n, o in enumerate(OFFSETS):
        p = to(o)
        send[n] = output(p)
        c = remote(send.at[n], got.at[d], os_sem.at[n], or_sem.at[n], z * GROUP + p)
        c.start()
        o_copies.append(c)
    got[d] = output(d)

    stores = []

    def finish(n, p):
        cols = columns(p)
        out[:, cols] = q[:, cols] * (got[p] + s[:, cols] * mix[p])
        c = pltpu.make_async_copy(out.at[:, cols], out_ref.at[:, cols], st_sem.at[n])
        c.start()
        stores.append(c)

    finish(GROUP - 1, d)
    for n, o in enumerate(OFFSETS):
        o_copies[n].wait_recv()
        finish(n, source(o))
    for c in f_copies + m_copies + h_copies + list(r_copies.values()) + o_copies:
        c.wait_send()
    for c in stores:
        c.wait()


def on_device(query_gate, key_gate, value_in, filters, skip_gain):
    width = GROUP * LANES
    hops = (NZ - 1) * PIECES
    arrays = [jnp.asarray(t) for t in tables()]
    vm = pltpu.VMEM
    dma = pltpu.SemaphoreType.DMA
    return pl.pallas_call(
        kernel,
        name="hyena",
        out_shape=jax.ShapeDtypeStruct((ROWS, width), F32),
        in_specs=[pl.BlockSpec(memory_space=pl.ANY)] * 9,
        out_specs=pl.BlockSpec(memory_space=pl.ANY),
        scratch_shapes=[
            vm((ROWS, width), F32),
            vm((ROWS, width), F32),
            vm((ROWS, width), F32),
            vm((LAGS, width), F32),
            vm((1, width), F32),
            vm((SPEC, ROWS), BF16),
            vm((SPEC, ROWS), BF16),
            vm((ROWS, SPEC), BF16),
            vm((ROWS, SPEC), BF16),
            vm((GROUP, ROWS, LANES), F32),
            vm((2 * GROUP, ROWS, LANES), F32),
            vm((NZ, ROWS, LANES), F32),
            vm((2 * GROUP, SPEC, LANES), F32),
            vm((NZ, SPEC, LANES), F32),
            vm((2 * GROUP - 1, SPEC, LANES), F32),
            vm((SPEC, LANES), F32),
            vm((GROUP - 1, ROWS, LANES), F32),
            vm((GROUP, ROWS, LANES), F32),
            vm((ROWS, width), F32),
            dma((9,)),
            dma((GROUP - 1,)), dma((GROUP - 1,)),
            dma((GROUP - 1,)), dma((GROUP - 1,)),
            dma((GROUP,)), dma((GROUP,)),
            dma((hops,)), dma((hops,)),
            dma((GROUP - 1,)), dma((GROUP - 1,)),
            dma((GROUP,)),
        ],
        compiler_params=pltpu.CompilerParams(
            collective_id=0, has_side_effects=True, vmem_limit_bytes=61 << 20
        ),
    )(key_gate, value_in, query_gate, filters, skip_gain.reshape(1, width), *arrays)


def solution(mesh):
    in_specs = (P("seq", "ch"), P("seq", "ch"), P("seq", "ch"), P("seq", "ch"), P("ch"))
    return jax.shard_map(
        on_device, mesh=mesh, in_specs=in_specs, out_specs=P("seq", "ch"), check_vma=False
    )
```

```python
import functools

import jax
import jax.numpy as jnp
import numpy as np
from jax import lax
from jax.experimental import pallas as pl
from jax.experimental.pallas import tpu as pltpu
from jax.sharding import PartitionSpec as P

MESH = pl.DeviceIdType.MESH
F32 = jnp.float32
BF16 = jnp.bfloat16
ROWS = 256
LANES = 128
NX, NY, NZ = 4, 2, 8
GROUP = NX * NY
LAGS = ROWS // GROUP
SPEC = 2 * ROWS
PIECES = 4
OFFSETS = [(0, 1), (0, 3), (1, 0), (1, 1), (1, 3), (0, 2), (1, 2)]


def tables():
    m = np.arange(ROWS)
    t = np.arange(ROWS)
    angle = np.pi * (((4 * m[:, None] + 1) * t[None, :]) % (4 * ROWS)) / (2 * ROWS)
    forward = np.concatenate([np.cos(angle), -np.sin(angle)], axis=0)
    back = np.concatenate([-np.sin(angle.T), -np.cos(angle.T)], axis=1) / ROWS
    split = []
    for table in (forward, back):
        high = table.astype(np.float32).astype(jnp.bfloat16)
        low = (table - high.astype(np.float64)).astype(np.float32).astype(jnp.bfloat16)
        split += [high, low]
    return split


def split(value):
    high = value.astype(BF16)
    low = (value - high.astype(F32)).astype(BF16)
    return high, low


def multiply(high_ref, low_ref, value):
    high, low = split(value)
    first = jnp.dot(high_ref[...], jnp.concatenate([high, low], axis=1), preferred_element_type=F32)
    second = jnp.dot(low_ref[...], high, preferred_element_type=F32)
    return first[:, :LANES] + first[:, LANES:] + second


def kernel(
    k_in, v_in, q_in, f_in, s_in, ch_in, cl_in, gh_in, gl_in, out_ref,
    k, v, q, f, s, ch, cl, gh, gl, mix, x, fb, y, fy, w, acc, send, got, out,
    load_sem, fs_sem, fr_sem, ms_sem, mr_sem, hs_sem, hr_sem, rs_sem, rr_sem, os_sem, or_sem, st_sem,
):
    seq = lax.axis_index("seq")
    z, d = seq // GROUP, seq % GROUP
    yy, xx = d // NX, d % NX
    above = ((z + 1) % NZ) * GROUP + d
    below = ((z + NZ - 1) % NZ) * GROUP + d

    def to(o):
        return ((yy + o[0]) % NY) * NX + (xx + o[1]) % NX

    def source(o):
        return ((yy + NY - o[0]) % NY) * NX + (xx + NX - o[1]) % NX

    def remote(src, dst, send_sem, recv_sem, dev):
        return pltpu.make_async_remote_copy(
            src_ref=src, dst_ref=dst, send_sem=send_sem, recv_sem=recv_sem,
            device_id={"seq": dev}, device_id_type=MESH,
        )

    def columns(p):
        return pl.ds(pl.multiple_of(p * LANES, LANES), LANES)

    loads = []
    for i, (a, b) in enumerate(
        [(f_in, f), (k_in, k), (v_in, v), (ch_in, ch), (cl_in, cl), (gh_in, gh), (gl_in, gl), (q_in, q), (s_in, s)]
    ):
        c = pltpu.make_async_copy(a, b, load_sem.at[i])
        c.start()
        loads.append(c)

    barrier = pltpu.get_barrier_semaphore()
    for o in OFFSETS:
        pl.semaphore_signal(barrier, inc=1, device_id={"seq": z * GROUP + to(o)}, device_id_type=MESH)
    for dev in (above, below):
        pl.semaphore_signal(barrier, inc=1, device_id={"seq": dev}, device_id_type=MESH)

    loads[0].wait()
    fb[z, pl.ds(pl.multiple_of(d * LAGS, LAGS), LAGS), :] = f[:, columns(d)]
    loads[1].wait()
    loads[2].wait()
    for p in range(GROUP):
        cols = slice(p * LANES, (p + 1) * LANES)
        mix[p] = k[:, cols] * v[:, cols]
    x[GROUP + d] = mix[d]
    pl.semaphore_wait(barrier, GROUP + 1)

    f_copies, m_copies = [], []
    for n, o in enumerate(OFFSETS):
        p = to(o)
        c = remote(
            f.at[:, columns(p)], fb.at[z, pl.ds(pl.multiple_of(d * LAGS, LAGS), LAGS)],
            fs_sem.at[n], fr_sem.at[n], z * GROUP + p,
        )
        c.start()
        f_copies.append(c)
    h_copies = []

    def halo(n, j):
        c = remote(x.at[GROUP + j], x.at[j], hs_sem.at[n], hr_sem.at[n], above)
        c.start()
        h_copies.append(c)

    halo(GROUP - 1, d)
    for n, o in enumerate(OFFSETS):
        p = to(o)
        c = remote(mix.at[p], x.at[GROUP + d], ms_sem.at[n], mr_sem.at[n], z * GROUP + p)
        c.start()
        m_copies.append(c)

    part = ROWS // PIECES
    r_copies = {}

    def hop(h, i):
        at = pl.ds(i * part, part)
        block = (z + h) % NZ
        c = remote(
            fb.at[block, at], fb.at[block, at], rs_sem.at[h * PIECES + i], rr_sem.at[h * PIECES + i], below
        )
        c.start()
        r_copies[h, i] = c

    def relay(h):
        for i in range(PIECES):
            r_copies[h, i].wait_recv()
            if h + 1 < NZ - 1:
                hop(h + 1, i)

    def arrive(n):
        m_copies[n].wait_recv()
        halo(n, source(OFFSETS[n]))

    def forward(src, block, dst, at):
        dst[at] = multiply(ch, cl, src[block])

    for c in f_copies:
        c.wait_recv()
    for i in range(PIECES):
        hop(0, i)
    for c in loads[3:]:
        c.wait()

    own = GROUP + d
    forward(x, own, y, own)
    forward(fb, z, fy, z)
    for h, group in enumerate([(0, 1), (2, 3), (4, 5), (6,)]):
        for n in group:
            arrive(n)
            j = GROUP + source(OFFSETS[n])
            forward(x, j, y, j)
        relay(h)
        block = (z + h + 1) % NZ
        forward(fb, block, fy, block)

    def window(n, carry):
        def tile(r, carry):
            at = pl.ds(pl.multiple_of(r * 16, 16), 16)
            im = pl.ds(pl.multiple_of(r * 16 + ROWS, 16), 16)
            w[n, at] = y[n, at] + y[n + 1, im]
            w[n, im] = y[n, im] - y[n + 1, at]
            return carry

        return lax.fori_loop(0, ROWS // 16, tile, carry, unroll=4)

    lax.fori_loop(GROUP, 2 * GROUP - 1, window, 0)
    inside = (z > 0).astype(F32)

    def take(n, j):
        h_copies_by_slot[n].wait_recv()
        y[j] = multiply(ch, cl, x[j] * inside)

    h_copies_by_slot = {}
    for n, c in zip([GROUP - 1] + list(range(GROUP - 1)), h_copies):
        h_copies_by_slot[n] = c

    take(GROUP - 1, d)
    take(0, source(OFFSETS[0]))
    for h in range(4, NZ - 1):
        relay(h)
        block = (z + h + 1) % NZ
        forward(fb, block, fy, block)
        n = h - 3
        take(n, source(OFFSETS[n]))
    for n in range(4, GROUP - 1):
        take(n, source(OFFSETS[n]))

    lax.fori_loop(0, GROUP, window, 0)

    def output(i):
        def tile(r, carry):
            at = pl.ds(pl.multiple_of(r * 8, 8), 8)
            im = pl.ds(pl.multiple_of(r * 8 + ROWS, 8), 8)
            real = jnp.zeros((8, LANES), F32)
            imag = jnp.zeros((8, LANES), F32)
            for j in range(GROUP):
                n = i + GROUP - 1 - j
                fr, fi = fy[j, at], fy[j, im]
                wr, wi = w[n, at], w[n, im]
                real += fr * wr - fi * wi
                imag += fr * wi + fi * wr
            acc[at] = real
            acc[im] = imag
            return carry

        lax.fori_loop(0, ROWS // 8, tile, 0, unroll=2)
        return multiply(gh, gl, acc[...])

    o_copies = []
    for n, o in enumerate(OFFSETS):
        p = to(o)
        send[n] = output(p)
        c = remote(send.at[n], got.at[d], os_sem.at[n], or_sem.at[n], z * GROUP + p)
        c.start()
        o_copies.append(c)
    got[d] = output(d)

    stores = []

    def finish(n, p):
        cols = columns(p)
        out[:, cols] = q[:, cols] * (got[p] + s[:, cols] * mix[p])
        c = pltpu.make_async_copy(out.at[:, cols], out_ref.at[:, cols], st_sem.at[n])
        c.start()
        stores.append(c)

    finish(GROUP - 1, d)
    for n, o in enumerate(OFFSETS):
        o_copies[n].wait_recv()
        finish(n, source(o))
    for c in f_copies + m_copies + h_copies + list(r_copies.values()) + o_copies:
        c.wait_send()
    for c in stores:
        c.wait()


def on_device(query_gate, key_gate, value_in, filters, skip_gain):
    width = GROUP * LANES
    hops = (NZ - 1) * PIECES
    arrays = [jnp.asarray(t) for t in tables()]
    vm = pltpu.VMEM
    dma = pltpu.SemaphoreType.DMA
    return pl.pallas_call(
        kernel,
        name="hyena",
        out_shape=jax.ShapeDtypeStruct((ROWS, width), F32),
        in_specs=[pl.BlockSpec(memory_space=pl.ANY)] * 9,
        out_specs=pl.BlockSpec(memory_space=pl.ANY),
        scratch_shapes=[
            vm((ROWS, width), F32),
            vm((ROWS, width), F32),
            vm((ROWS, width), F32),
            vm((LAGS, width), F32),
            vm((1, width), F32),
            vm((SPEC, ROWS), BF16),
            vm((SPEC, ROWS), BF16),
            vm((ROWS, SPEC), BF16),
            vm((ROWS, SPEC), BF16),
            vm((GROUP, ROWS, LANES), F32),
            vm((2 * GROUP, ROWS, LANES), F32),
            vm((NZ, ROWS, LANES), F32),
            vm((2 * GROUP, SPEC, LANES), F32),
            vm((NZ, SPEC, LANES), F32),
            vm((2 * GROUP - 1, SPEC, LANES), F32),
            vm((SPEC, LANES), F32),
            vm((GROUP - 1, ROWS, LANES), F32),
            vm((GROUP, ROWS, LANES), F32),
            vm((ROWS, width), F32),
            dma((9,)),
            dma((GROUP - 1,)), dma((GROUP - 1,)),
            dma((GROUP - 1,)), dma((GROUP - 1,)),
            dma((GROUP,)), dma((GROUP,)),
            dma((hops,)), dma((hops,)),
            dma((GROUP - 1,)), dma((GROUP - 1,)),
            dma((GROUP,)),
        ],
        compiler_params=pltpu.CompilerParams(
            collective_id=0, has_side_effects=True, vmem_limit_bytes=61 << 20
        ),
    )(key_gate, value_in, query_gate, filters, skip_gain.reshape(1, width), *arrays)


def solution(mesh):
    in_specs = (P("seq", "ch"), P("seq", "ch"), P("seq", "ch"), P("seq", "ch"), P("ch"))
    return jax.shard_map(
        on_device, mesh=mesh, in_specs=in_specs, out_specs=P("seq", "ch"), check_vma=False
    )
```
